256 devices in a mesh: row: 16 (over x, y_hi, core), col: 16 (over y_lo, z).
Axes of the slice: x: 4, y: 4 (y_hi: 2, y_lo: 2; y = y_hi * 2 + y_lo), z: 8, core: 2. Of those that a mesh axis runs over, the one named last changes fastest.
Arguments:
- matrix: float32 [16, 3, 256, 16, 3, 256], P('row', None, None, 'col'), as said below
- checksum: float32 [16, 3, 256, 3, 256], P('row'), as said below
- failed: int32 [16], P('col'), may hold values from 0 to 15, as said below
Outputs:
- factored: float32 [16, 3, 256, 16, 3, 256], P('row', None, None, 'col')
- updated_checksum_result: float32 [16, 3, 256, 3, 256], P('row')
The draws below stay inside these ranges and needn't reach their ends.
Inputs may be any that keep to these rules, and one draw needn't show every extreme that they name: `failed`: a permutation of the grid column indices; entry 0 names the grid column whose tiles in matrix carry no information. With the lost grid column rebuilt from checksum, matrix is symmetric positive definite. `checksum`: for each grid row, the sum over all grid columns of the intact matrix's tiles, the lost column included.
All inputs are finite; a program needn't handle non-finite values.
Results may differ from the reference program's by a relative error of at most 0.0003.
Values sent between devices are 32-bit elements; how exact they have to be, the bound alone decides.
No kernel may reach another device: no remote copies, remote signals or barrier semaphores. Data moves between devices by JAX's collectives and lax.ppermute only.
A program may use at most 128 MiB of HBM per device.

```python
import math
import jax
import jax.numpy as jnp
from jax import lax

B = 256
PANELS = 3
GRID_ROWS = 16
GRID_COLS = 16
NT = 48
TR = 3
TC = 3
ORDER = 12288


def intact_tiles(key):
    full_order = NT * B
    inner_width = 2 * B
    loadings = jax.random.normal(jax.random.fold_in(key, 5), (full_order, inner_width), jnp.float32)
    loadings = loadings / math.sqrt(inner_width)
    square = 2.0 * jnp.dot(loadings, loadings.T, precision=lax.Precision.HIGHEST)
    diagonal_lift = jax.random.uniform(jax.random.fold_in(key, 6), (full_order,), jnp.float32, 0.5, 1.5)
    square = square + jnp.diag(diagonal_lift)
    return square.reshape(TR, GRID_ROWS, B, TC, GRID_COLS, B).transpose(1, 0, 2, 4, 3, 5)


def column_order(key):
    return jax.random.permutation(jax.random.fold_in(key, 4517), jnp.arange(GRID_COLS, dtype=jnp.int32))


def draw_failed(key, part):
    return column_order(key)


def draw_matrix(key, part):
    blocks = intact_tiles(key)
    garbage = jax.random.normal(jax.random.fold_in(key, 7), blocks.shape, jnp.float32)
    column_ids = jnp.arange(GRID_COLS, dtype=jnp.int32).reshape(1, 1, 1, GRID_COLS, 1, 1)
    return jnp.where(column_ids == column_order(key)[0], garbage, blocks)


def draw_checksum(key, part):
    return jnp.sum(intact_tiles(key), axis=3)


def setup_inputs(seed: int = 0) -> dict:
    streams_of = jax.random.split(jax.random.key(seed), 4)
    return {
        "matrix": draw_matrix(jax.random.fold_in(streams_of[3], 71), 0),
        "checksum": draw_checksum(jax.random.fold_in(streams_of[3], 71), 0),
        "failed": draw_failed(jax.random.fold_in(streams_of[3], 71), 0),
    }


def to_natural(blocks):
    return blocks.transpose(1, 0, 2, 4, 3, 5).reshape(ORDER, ORDER)

def split_into_tiles(square):
    return square.reshape(TR, GRID_ROWS, B, TC, GRID_COLS, B).transpose(1, 0, 2, 4, 3, 5)

def reference(matrix, checksum, failed):
    missing_tiles = failed[0]
    column_ids = jnp.arange(GRID_COLS, dtype=jnp.int32).reshape(1, 1, 1, GRID_COLS, 1, 1)
    remaining_peers = jnp.sum(jnp.where(column_ids != missing_tiles, matrix, 0.0), axis=3)
    restored_tiles = jnp.where(column_ids == missing_tiles, (checksum - remaining_peers)[:, :, :, None], matrix)
    work = to_natural(restored_tiles)
    columns = []
    for panel in range(PANELS):
        start = panel * B
        factor = jnp.linalg.cholesky(work[start:start + B, start:start + B])
        below = work[start + B:, start:start + B]
        solved = jax.scipy.linalg.solve_triangular(factor, below.T, lower=True).T
        upper_zero = jnp.zeros((start, B), work.dtype)
        block_column = jnp.concatenate([upper_zero, factor, solved], axis=0)
        work = work - jnp.dot(block_column, block_column.T, precision=lax.Precision.HIGHEST)
        columns.append(block_column)
    tiles = split_into_tiles(work)
    updated_checksum_result = jnp.sum(tiles, axis=3)
    for panel in range(PANELS):
        panel_tiles = columns[panel].reshape(TR, GRID_ROWS, B, B).transpose(1, 0, 2, 3)
        tiles = tiles.at[:, :, :, panel % GRID_COLS, panel // GRID_COLS, :].set(panel_tiles)
    tile_rows = jnp.arange(GRID_ROWS)[:, None] + jnp.arange(TR)[None, :] * GRID_ROWS
    tile_cols = jnp.arange(GRID_COLS)[:, None] + jnp.arange(TC)[None, :] * GRID_COLS
    keep = tile_rows.reshape(GRID_ROWS, TR, 1, 1, 1, 1) >= tile_cols.reshape(1, 1, 1, GRID_COLS, TC, 1)
    factored = jnp.where(keep, tiles, 0.0)
    return (factored, updated_checksum_result)
```

```python
import jax
import jax.numpy as jnp
from jax import lax
from jax.sharding import Mesh
from jax.sharding import PartitionSpec as P

PANELS = 3
COL = ("col_0", "col_1")
HIGHEST = lax.Precision.HIGHEST


def gather_by_exchange(x, axis):
    peers = lax.axis_size(axis)
    return lax.all_to_all(jnp.broadcast_to(x[None], (peers, *x.shape)), axis, 0, 0, tiled=True)


def mm(a, b):
    return jnp.dot(a, b, precision=HIGHEST)


def mm_t(a, b):
    return lax.dot_general(a, b, (((1,), (1,)), ((), ())), precision=HIGHEST)


def factor_lead(lead, width):
    eye = jnp.eye(width, dtype=jnp.float32)
    tile = lambda i, j: lead[i * width : (i + 1) * width, j * width : (j + 1) * width]
    blocks = {(i, j): tile(i, j) for i in range(PANELS) for j in range(i + 1)}
    inverses = []
    for k in range(PANELS):
        factor = jnp.linalg.cholesky(blocks[k, k])
        inverse = jax.scipy.linalg.solve_triangular(factor, eye, lower=True)
        inverses.append(inverse)
        for i in range(k + 1, PANELS):
            blocks[i, k] = mm_t(blocks[i, k], inverse)
        for i in range(k + 1, PANELS):
            for j in range(k + 1, i + 1):
                blocks[i, j] = blocks[i, j] - mm_t(blocks[i, k], blocks[j, k])
    return blocks, inverses


def solve_rows(rows, blocks, inverses, width):
    out = []
    for k in range(PANELS):
        part = rows[:, k * width : (k + 1) * width]
        for m in range(k):
            part = part - mm_t(out[m], blocks[k, m])
        out.append(mm_t(part, inverses[k]))
    return jnp.concatenate(out, axis=1)


def solve_columns(columns, blocks, inverses, width):
    out = []
    for k in range(PANELS):
        part = columns[k * width : (k + 1) * width]
        for m in range(k):
            part = part - mm(blocks[k, m], out[m])
        out.append(mm(inverses[k], part))
    return jnp.concatenate(out, axis=0)


def shards(matrix, checksum, failed):
    rows_count = lax.axis_size("row")
    cols_count = lax.axis_size(COL)
    p = lax.axis_index("row")
    q = lax.axis_index(COL)
    tr, width, tc = (matrix.shape[1], matrix.shape[2], matrix.shape[4])
    tiles = matrix.reshape(tr, width, tc, width)
    checks = checksum.reshape(tr, width, tc, width)
    piece = width // cols_count
    missing = gather_by_exchange(failed, COL).reshape(-1)[0]

    first = tiles[:, :, 0, :].reshape(tr, cols_count, piece, width).transpose(1, 0, 2, 3)
    parts = lax.all_to_all(first, COL, 0, 0, tiled=True)
    members = jnp.arange(cols_count)[:, None, None, None]
    healthy = jnp.sum(jnp.where(members != missing, parts, 0.0), axis=0)
    check_piece = lax.dynamic_slice_in_dim(checks, q * piece, piece, 1)
    rebuilt = check_piece[:, :, 0, :] - healthy
    panel_piece = jnp.concatenate(
        [jnp.where(missing == k, rebuilt, parts[k]) for k in range(PANELS)], axis=-1
    )

    both = jnp.stack([panel_piece[0], check_piece[0].reshape(piece, tc * width)])
    both = gather_by_exchange(both, "row")[:PANELS]
    lead = gather_by_exchange(both[:, 0], COL)
    lead = lead.transpose(1, 0, 2, 3).reshape(PANELS * width, PANELS * width)
    top = lax.all_gather(both[:, 1], COL)
    top = top.transpose(1, 0, 2, 3).reshape(PANELS * width, tc * width)

    row_panel = lax.all_gather(panel_piece, COL)
    row_panel = row_panel.transpose(1, 0, 2, 3).reshape(tr * width, PANELS * width)
    swap = [(i * cols_count + j, j * cols_count + i) for i in range(rows_count) for j in range(cols_count)]
    col_piece = lax.ppermute(panel_piece, ("row",) + COL, swap)
    col_panel = lax.all_gather(col_piece, "row")
    col_panel = col_panel.transpose(1, 0, 2, 3).reshape(tc * width, PANELS * width)

    lower = [(a, b) for a in range(tr) for b in range(min(a + 1, tc))]
    stacked = jnp.stack([tiles[a, :, b, :] for a, b in lower])
    others = lax.psum(jnp.where(q != missing, stacked, 0.0), COL)
    held = jnp.stack([checks[a, :, b, :] for a, b in lower]) - others
    work = jnp.where(q == missing, held, stacked)

    blocks, inverses = factor_lead(lead, width)
    x_rows = solve_rows(row_panel, blocks, inverses, width)
    x_cols = solve_rows(col_panel, blocks, inverses, width)
    sums = solve_columns(top, blocks, inverses, width)

    totals = checks.reshape(tr * width, tc * width) - mm(x_rows, sums)

    triangle = jnp.tril(jnp.ones((width, width), jnp.bool_))
    zero = jnp.zeros((width, width), jnp.float32)
    columns = [[zero] * tr for _ in range(tc)]
    for n, (a, b) in enumerate(lower):
        i, j = p + a * rows_count, q + b * cols_count
        x_a = x_rows[a * width : (a + 1) * width]
        tile = work[n] - mm_t(x_a, x_cols[b * width : (b + 1) * width])
        for k in range(b * cols_count, min(PANELS, (b + 1) * cols_count)):
            own = x_a[:, k * width : (k + 1) * width]
            own = jnp.where(jnp.logical_or(i > k, triangle), own, 0.0)
            tile = jnp.where(j == k, own, tile)
        columns[b][a] = jnp.where(i >= j, tile, 0.0)
    factored = jnp.stack([jnp.stack(c, axis=0) for c in columns], axis=2)
    return (factored.reshape(matrix.shape), totals.reshape(checksum.shape))


def solution(mesh):
    finer = Mesh(mesh.devices.reshape(mesh.shape["row"], 2, 8), ("row", "col_0", "col_1"))
    in_specs = (P("row", None, None, COL, None, None), P("row", None, None, None, None), P(COL))
    out_specs = (P("row", None, None, COL, None, None), P("row", None, None, None, None))
    return jax.shard_map(
        shards, mesh=finer, in_specs=in_specs, out_specs=out_specs, check_vma=False
    )
```

```python
import jax
import jax.numpy as jnp
from jax import lax
from jax.experimental import pallas as pl
from jax.experimental.pallas import tpu as pltpu
from jax.sharding import Mesh
from jax.sharding import PartitionSpec as P

PANELS = 3
COL = ("col_0", "col_1")
LOWER = [(0, 0), (1, 0), (1, 1), (2, 0), (2, 1), (2, 2)]
F32 = jnp.float32
VMEM = pl.BlockSpec(memory_space=pltpu.VMEM)
SMEM = pl.BlockSpec(memory_space=pltpu.SMEM)
PARAMS = pltpu.CompilerParams(vmem_limit_bytes=48 << 20)


def mm(a, b):
    return lax.dot_general(
        a, b, (((1,), (0,)), ((), ())), precision=lax.Precision.HIGHEST, preferred_element_type=F32
    )


def mm_t(a, b):
    return lax.dot_general(
        a, b, (((1,), (1,)), ((), ())), precision=lax.Precision.HIGHEST, preferred_element_type=F32
    )


def base_inverse(a):
    n = a.shape[0]
    groups = n // 8
    rows = lax.broadcasted_iota(jnp.int32, (8, n), 0)
    lanes = lax.broadcasted_iota(jnp.int32, (8, n), 1)
    ag = [a[8 * g : 8 * g + 8, :] for g in range(groups)]
    mg = [jnp.where(lanes == rows + 8 * g, 1.0, 0.0).astype(F32) for g in range(groups)]
    for m in range(groups):
        columns = [
            [
                jnp.broadcast_to(ag[g][:, 8 * m + k : 8 * m + k + 1], (8, n))
                for g in range(m, groups)
            ]
            for k in range(8)
        ]
        top, mine = ag[m], mg[m]
        us, vs, ls = [], [], []
        for k in range(8):
            scale = lax.rsqrt(columns[k][0][k : k + 1, :])
            l = [x * scale for x in columns[k]]
            for k2 in range(k + 1, 8):
                s = l[0][k2 : k2 + 1, :]
                columns[k2] = [x - y * s for x, y in zip(columns[k2], l)]
            u = top[k : k + 1, :] * scale
            v = mine[k : k + 1, :] * scale
            below = jnp.where(rows > k, l[0], 0.0)
            top = top - below * u
            mine = jnp.where(rows == k, v, mine - below * v)
            us.append(u)
            vs.append(v)
            ls.append(l[1:])
        mg[m] = mine
        for t, g in enumerate(range(m + 1, groups)):
            ag[g] = ag[g] - sum(ls[k][t] * us[k] for k in range(8))
            mg[g] = mg[g] - sum(ls[k][t] * vs[k] for k in range(8))
    return jnp.concatenate(mg, axis=0)


def tile_inverse(a):
    h = a.shape[0] // 2
    first = base_inverse(a[:h, :h])
    l10 = mm_t(a[h:, :h], first)
    second = base_inverse(a[h:, h:] - mm_t(l10, l10))
    low = -mm(second, mm(l10, first))
    return jnp.concatenate(
        [
            jnp.concatenate([first, jnp.zeros_like(first)], 1),
            jnp.concatenate([low, second], 1),
        ],
        0,
    )


def whole(ref, n):
    t = ref[:, n]
    return t.reshape(t.shape[0] * t.shape[1], t.shape[2])


def lead_kernel(t_ref, off_ref, inv_ref):
    tile = lambda n: whole(t_ref, n)
    i0 = tile_inverse(tile(0))
    inv_ref[0] = i0
    l10 = mm_t(tile(1), i0)
    off_ref[0] = l10
    i1 = tile_inverse(tile(2) - mm_t(l10, l10))
    inv_ref[1] = i1
    l20 = mm_t(tile(3), i0)
    off_ref[1] = l20
    l21 = mm_t(tile(4) - mm_t(l20, l10), i1)
    off_ref[2] = l21
    inv_ref[2] = tile_inverse(tile(5) - mm_t(l20, l20) - mm_t(l21, l21))


def tile_rows(a, b, half):
    return pl.ds(a * 1536 + 2 * b + half, 256, stride=6)


def prepare_kernel(m_ref, c_ref, f_ref, col_ref, row_ref):
    for n, (a, b) in enumerate(LOWER):
        for half in range(2):
            lanes = slice(128 * half, 128 * half + 128)
            v = m_ref[tile_rows(a, b, half), :].reshape(16, 16, 128)
            col_ref[:, 16 * n : 16 * n + 16, lanes] = v
            if n == 0:
                row_ref[:, 0:16, lanes] = v
    col_ref[:, 96:104, :] = jnp.full((16, 8, 256), f_ref[0].astype(F32))
    for b in range(3):
        row_ref[:, 16 * b + 16 : 16 * b + 32, :] = c_ref[0, b].reshape(16, 16, 256)


def fix_lead_kernel(g_ref, r_ref, out_ref):
    missing = g_ref[0, 48:49, :]
    rebuilt = []
    for i in range(PANELS):
        part = slice(16 * i, 16 * i + 16)
        healthy = jnp.zeros((16, 256), F32)
        for j in range(16):
            healthy = healthy + jnp.where(missing != float(j), g_ref[j, part, :], 0.0)
        rebuilt.append(r_ref[i, 16:32, :] - healthy)
    for n, (i, k) in enumerate(LOWER):
        v = jnp.where(missing == float(k), rebuilt[i], g_ref[k, 16 * i : 16 * i + 16, :])
        for s in range(16):
            out_ref[s, n] = v


def fix_columns_kernel(g_ref, c_ref, send_ref, panel_ref, lost_ref):
    missing = g_ref[0, 96:97, :]
    for n, (a, b) in enumerate(LOWER):
        part = slice(16 * n, 16 * n + 16)
        healthy = jnp.zeros((16, 256), F32)
        for j in range(16):
            healthy = healthy + jnp.where(missing != float(j), g_ref[j, part, :], 0.0)
        rebuilt = c_ref[a, b] - healthy
        lost_ref[n] = rebuilt
        if b == 0:
            for k in range(PANELS):
                v = jnp.where(missing == float(k), rebuilt, g_ref[k, part, :])
                panel_ref[3 * a + k] = v
                for s in range(16):
                    send_ref[s, 3 * a + k] = v


def finish_kernel(
    place_ref, r_ref, q_ref, k_ref, d_ref, m_ref, c_ref, off_ref, inv_ref,
    f_ref, t_ref, x_ref, y_ref, s_ref,
):
    p, q, missing = place_ref[0], place_ref[1], place_ref[2]

    for source, target in ((r_ref, x_ref), (q_ref, y_ref)):

        @pl.loop(0, 3)
        def _(a, source=source, target=target):
            x0 = mm_t(whole(source, 3 * a), inv_ref[0])
            target[a, 0] = x0
            x1 = mm_t(whole(source, 3 * a + 1) - mm_t(x0, off_ref[0]), inv_ref[1])
            target[a, 1] = x1
            rest = whole(source, 3 * a + 2) - mm_t(x0, off_ref[1]) - mm_t(x1, off_ref[2])
            target[a, 2] = mm_t(rest, inv_ref[2])

    @pl.loop(0, 3)
    def _(b):
        s0 = mm(inv_ref[0], whole(k_ref, b))
        s_ref[b, 0] = s0
        s1 = mm(inv_ref[1], whole(k_ref, 3 + b) - mm(off_ref[0], s0))
        s_ref[b, 1] = s1
        rest = whole(k_ref, 6 + b) - mm(off_ref[1], s0) - mm(off_ref[2], s1)
        s_ref[b, 2] = mm(inv_ref[2], rest)

    @pl.loop(0, 9)
    def _(n):
        a, b = n // 3, n % 3
        total = c_ref[a, b]
        for k in range(PANELS):
            total = total - mm(x_ref[a, k], s_ref[b, k])
        t_ref[a, b] = total

    def store(a, b, value):
        for half in range(2):
            f_ref[tile_rows(a, b, half), :] = value[:, 128 * half : 128 * half + 128]

    for n, (a, b) in enumerate(LOWER):
        i, j = p + 16 * a, q + 16 * b
        kept = i >= j
        panel = jnp.logical_and(kept, j < PANELS) if b == 0 else jnp.bool_(False)
        inner = jnp.logical_and(kept, jnp.logical_not(panel))

        @pl.when(jnp.logical_not(kept))
        def _():
            store(a, b, jnp.zeros((256, 256), F32))

        if b == 0:

            @pl.when(panel)
            def _():
                value = x_ref[a, jnp.minimum(q, PANELS - 1)]
                rows = lax.broadcasted_iota(jnp.int32, (256, 256), 0)
                cols = lax.broadcasted_iota(jnp.int32, (256, 256), 1)
                value = jnp.where(jnp.logical_or(rows >= cols, i > q), value, 0.0)
                store(a, b, value)

        @pl.when(inner)
        def _():
            update = mm_t(x_ref[a, 0], y_ref[b, 0])
            update = update + mm_t(x_ref[a, 1], y_ref[b, 1])
            update = update + mm_t(x_ref[a, 2], y_ref[b, 2])

            @pl.when(q == missing)
            def _():
                store(a, b, whole(d_ref, n) - update)

            @pl.when(q != missing)
            def _():
                for half in range(2):
                    rows = tile_rows(a, b, half)
                    f_ref[rows, :] = m_ref[rows, :] - update[:, 128 * half : 128 * half + 128]

    for a, b in ((0, 1), (0, 2), (1, 2)):
        store(a, b, jnp.zeros((256, 256), F32))


def call(kernel, outs, ins, specs=None, scratch=()):
    shapes = [jax.ShapeDtypeStruct(s, F32) for s in outs]
    return pl.pallas_call(
        kernel,
        out_shape=shapes,
        in_specs=specs or [VMEM] * len(ins),
        out_specs=[VMEM] * len(outs),
        scratch_shapes=[pltpu.VMEM(s, F32) for s in scratch],
        compiler_params=PARAMS,
    )(*ins)


def exchange(x, axis):
    return lax.all_to_all(x, axis, 0, 0, tiled=True)


def to_all(x, axis):
    return exchange(jnp.broadcast_to(x[None], (16, *x.shape)), axis)


def shards(matrix, checksum, failed):
    p = lax.axis_index("row")
    q = lax.axis_index(COL)
    block = matrix.reshape(4608, 128)
    checks = checksum.reshape(3, 256, 3, 256).transpose(0, 2, 1, 3)

    col_send, row_send = call(
        prepare_kernel, [(16, 104, 256), (16, 64, 256)], [block, checks, failed], [VMEM, VMEM, SMEM]
    )
    row_got = exchange(row_send, "row")
    col_got = exchange(col_send, COL)

    first = jnp.concatenate(
        [row_got[:PANELS, :16].reshape(48, 256), jnp.full((8, 256), failed[0].astype(F32))]
    )
    first = to_all(first, COL)
    (lead_send,) = call(fix_lead_kernel, [(16, 6, 16, 256)], [first, row_got[:PANELS]])
    lead = exchange(lead_send, "row")

    top = to_all(row_got[:PANELS, 16:].reshape(9, 16, 256), "row")

    check_piece = lax.dynamic_slice_in_dim(checks, q * 16, 16, 2)
    panel_send, panel_piece, lost_piece = call(
        fix_columns_kernel,
        [(16, 9, 16, 256), (9, 16, 256), (6, 16, 256)],
        [col_got, check_piece],
    )
    row_panel = exchange(panel_send, COL)
    swap = [(i * 16 + j, j * 16 + i) for i in range(16) for j in range(16)]
    col_panel = to_all(lax.ppermute(panel_piece, ("row",) + COL, swap), "row")
    lost = lax.all_gather(lost_piece, COL)

    tiles = [(PANELS, 256, 256)] * 2
    off, inv = call(lead_kernel, tiles, [lead])

    missing = col_got[0, 96, 0].astype(jnp.int32)
    place = jnp.stack([p, q, missing]).astype(jnp.int32)
    factored, totals = call(
        finish_kernel,
        [(4608, 128), (3, 3, 256, 256)],
        [place, row_panel, col_panel, top, lost, block, checks, off, inv],
        [SMEM] + [VMEM] * 8,
        [(3, 3, 256, 256)] * 3,
    )
    totals = totals.transpose(0, 2, 1, 3).reshape(checksum.shape)
    return (factored.reshape(matrix.shape), totals)


def solution(mesh):
    finer = Mesh(mesh.devices.reshape(mesh.shape["row"], 2, 8), ("row", "col_0", "col_1"))
    in_specs = (P("row", None, None, COL, None, None), P("row", None, None, None, None), P(COL))
    out_specs = (P("row", None, None, COL, None, None), P("row", None, None, None, None))
    return jax.shard_map(
        shards, mesh=finer, in_specs=in_specs, out_specs=out_specs, check_vma=False
    )
```

```python
import jax
import jax.numpy as jnp
from jax import lax
from jax.experimental import pallas as pl
from jax.experimental.pallas import tpu as pltpu
from jax.sharding import Mesh
from jax.sharding import PartitionSpec as P

PANELS = 3
ROW = ("xy", "core")
COL = ("col_0", "col_1")
LOWER = [(0, 0), (1, 0), (1, 1), (2, 0), (2, 1), (2, 2)]
F32 = jnp.float32
VMEM = pl.BlockSpec(memory_space=pltpu.VMEM)
SMEM = pl.BlockSpec(memory_space=pltpu.SMEM)
PARAMS = pltpu.CompilerParams(vmem_limit_bytes=48 << 20)


def mm(a, b):
    return lax.dot_general(
        a, b, (((1,), (0,)), ((), ())), precision=lax.Precision.HIGHEST, preferred_element_type=F32
    )


def mm_t(a, b):
    return lax.dot_general(
        a, b, (((1,), (1,)), ((), ())), precision=lax.Precision.HIGHEST, preferred_element_type=F32
    )


def halves(x):
    high = x.astype(jnp.bfloat16)
    return high, (x - high.astype(F32)).astype(jnp.bfloat16)


def split_dot(a, b, dims):
    (ah, al), (bh, bl) = halves(a), halves(b)
    dot = lambda u, v: lax.dot_general(u, v, (dims, ((), ())), preferred_element_type=F32)
    return dot(ah, bh) + (dot(ah, bl) + dot(al, bh))


def mm3(a, b):
    return split_dot(a, b, ((1,), (0,)))


def mm3_t(a, b):
    return split_dot(a, b, ((1,), (1,)))


def base_inverse(a):
    n = a.shape[0]
    groups = n // 8
    rows = lax.broadcasted_iota(jnp.int32, (8, n), 0)
    lanes = lax.broadcasted_iota(jnp.int32, (8, n), 1)
    ag = [a[8 * g : 8 * g + 8, :] for g in range(groups)]
    mg = [jnp.where(lanes == rows + 8 * g, 1.0, 0.0).astype(F32) for g in range(groups)]
    for m in range(groups):
        columns = [
            [
                jnp.broadcast_to(ag[g][:, 8 * m + k : 8 * m + k + 1], (8, n))
                for g in range(m, groups)
            ]
            for k in range(8)
        ]
        top, mine = ag[m], mg[m]
        us, vs, ls = [], [], []
        for k in range(8):
            scale = lax.rsqrt(columns[k][0][k : k + 1, :])
            l = [x * scale for x in columns[k]]
            for k2 in range(k + 1, 8):
                s = l[0][k2 : k2 + 1, :]
                columns[k2] = [x - y * s for x, y in zip(columns[k2], l)]
            u = top[k : k + 1, :] * scale
            v = mine[k : k + 1, :] * scale
            below = jnp.where(rows > k, l[0], 0.0)
            top = top - below * u
            mine = jnp.where(rows == k, v, mine - below * v)
            us.append(u)
            vs.append(v)
            ls.append(l[1:])
        mg[m] = mine
        for t, g in enumerate(range(m + 1, groups)):
            ag[g] = ag[g] - sum(ls[k][t] * us[k] for k in range(8))
            mg[g] = mg[g] - sum(ls[k][t] * vs[k] for k in range(8))
    return jnp.concatenate(mg, axis=0)


def tile_inverse(a):
    h = a.shape[0] // 2
    first = base_inverse(a[:h, :h])
    l10 = mm_t(a[h:, :h], first)
    second = base_inverse(a[h:, h:] - mm_t(l10, l10))
    low = -mm(second, mm(l10, first))
    return jnp.concatenate(
        [
            jnp.concatenate([first, jnp.zeros_like(first)], 1),
            jnp.concatenate([low, second], 1),
        ],
        0,
    )


def whole(ref, n):
    t = ref[:, n]
    return t.reshape(t.shape[0] * t.shape[1], t.shape[2])


def woven(even, odd, n):
    t = jnp.stack([even[:, n], odd[:, n]], axis=1)
    return t.reshape(256, 256)


def by_core(core, mine_ref, other_ref, body):
    @pl.when(core == 0)
    def _():
        body(mine_ref, other_ref)

    @pl.when(core != 0)
    def _():
        body(other_ref, mine_ref)


def lead_kernel(core_ref, mine_ref, other_ref, off_ref, inv_ref, t_ref):
    def gather(even, odd):
        for n in range(6):
            t_ref[n] = woven(even, odd, n)

    by_core(core_ref[0], mine_ref, other_ref, gather)
    i0 = tile_inverse(t_ref[0])
    inv_ref[0] = i0
    l10 = mm_t(t_ref[1], i0)
    off_ref[0] = l10
    i1 = tile_inverse(t_ref[2] - mm_t(l10, l10))
    inv_ref[1] = i1
    l20 = mm_t(t_ref[3], i0)
    off_ref[1] = l20
    l21 = mm_t(t_ref[4] - mm_t(l20, l10), i1)
    off_ref[2] = l21
    inv_ref[2] = tile_inverse(t_ref[5] - mm_t(l20, l20) - mm_t(l21, l21))


def tile_rows(a, b, half):
    return pl.ds(a * 1536 + 2 * b + half, 256, stride=6)


def prepare_kernel(m_ref, f_ref, col_ref):
    for n, (a, b) in enumerate(LOWER):
        for half in range(2):
            v = m_ref[tile_rows(a, b, half), :].reshape(16, 16, 128)
            col_ref[:, 16 * n : 16 * n + 16, 128 * half : 128 * half + 128] = v
    col_ref[:, 96:104, :] = jnp.full((16, 8, 256), f_ref[0].astype(F32))


def rebuild_kernel(g_ref, c_ref, panel_ref, lost_ref, send_ref):
    missing = g_ref[0, 96:97, :]
    for n, (a, b) in enumerate(LOWER):
        part = slice(16 * n, 16 * n + 16)
        healthy = jnp.zeros((16, 256), F32)
        for j in range(16):
            healthy = healthy + jnp.where(missing != float(j), g_ref[j, part, :], 0.0)
        rebuilt = c_ref[a, b] - healthy
        lost_ref[n] = rebuilt
        if b == 0:
            for k in range(PANELS):
                v = jnp.where(missing == float(k), rebuilt, g_ref[k, part, :])
                panel_ref[3 * a + k] = v
                if a == 0:
                    for s in range(16):
                        send_ref[s, k] = v


def lead_half_kernel(core_ref, g_ref, send_ref):
    rows = pl.ds(pl.multiple_of(8 * core_ref[0], 8), 8)
    for n, (i, k) in enumerate(LOWER):
        v = g_ref[i, k, rows, :]
        for s in range(16):
            send_ref[s, n] = v


def finish_kernel(
    place_ref, r_ref, mine_ref, other_ref, top_mine_ref, top_other_ref, near_ref, far_ref,
    m_ref, c_ref, off_ref, inv_ref,
    f_ref, t_ref, x_ref, y_ref, s_ref, q_ref, k_ref, d_ref,
):
    p, q, missing = place_ref[0], place_ref[1], place_ref[2]

    core, chip = lax.rem(p, 2), p // 2

    def gather(even, odd):
        for n in range(9):
            q_ref[n] = woven(even, odd, n)

    by_core(core, mine_ref, other_ref, gather)

    for s in range(8):
        source = lax.bitwise_xor(chip, s)
        for ref, half in ((top_mine_ref, core), (top_other_ref, 1 - core)):
            rows = pl.ds(pl.multiple_of(32 * source + 16 * half, 16), 16)
            for n in range(9):
                k_ref[n, rows, :] = ref[s, n]

    @pl.when(q == missing)
    def _():
        y, z = q // 8, lax.rem(q, 8)
        for s in range(8):
            source = lax.rem(z - s + 8, 8)
            for ref, half in ((near_ref, y), (far_ref, 1 - y)):
                rows = pl.ds(pl.multiple_of(16 * (8 * half + source), 16), 16)
                for n in range(6):
                    d_ref[n, rows, :] = ref[s, n]

    for source, target in ((lambda n: whole(r_ref, n), x_ref), (lambda n: q_ref[n], y_ref)):

        @pl.loop(0, 3)
        def _(a, source=source, target=target):
            x0 = mm3_t(source(3 * a), inv_ref[0])
            target[a, 0] = x0
            x1 = mm3_t(source(3 * a + 1) - mm3_t(x0, off_ref[0]), inv_ref[1])
            target[a, 1] = x1
            rest = source(3 * a + 2) - mm3_t(x0, off_ref[1]) - mm3_t(x1, off_ref[2])
            target[a, 2] = mm3_t(rest, inv_ref[2])

    @pl.loop(0, 3)
    def _(b):
        s0 = mm3(inv_ref[0], k_ref[b])
        s_ref[b, 0] = s0
        s1 = mm3(inv_ref[1], k_ref[3 + b] - mm3(off_ref[0], s0))
        s_ref[b, 1] = s1
        rest = k_ref[6 + b] - mm3(off_ref[1], s0) - mm3(off_ref[2], s1)
        s_ref[b, 2] = mm3(inv_ref[2], rest)

    @pl.loop(0, 9)
    def _(n):
        a, b = n // 3, n % 3
        total = c_ref[a, b]
        for k in range(PANELS):
            total = total - mm3(x_ref[a, k], s_ref[b, k])
        t_ref[a, b] = total

    def store(a, b, value):
        for half in range(2):
            f_ref[tile_rows(a, b, half), :] = value[:, 128 * half : 128 * half + 128]

    for n, (a, b) in enumerate(LOWER):
        i, j = p + 16 * a, q + 16 * b
        kept = i >= j
        panel = jnp.logical_and(kept, j < PANELS) if b == 0 else jnp.bool_(False)
        inner = jnp.logical_and(kept, jnp.logical_not(panel))

        @pl.when(jnp.logical_not(kept))
        def _():
            store(a, b, jnp.zeros((256, 256), F32))

        if b == 0:

            @pl.when(panel)
            def _():
                value = x_ref[a, jnp.minimum(q, PANELS - 1)]
                rows = lax.broadcasted_iota(jnp.int32, (256, 256), 0)
                cols = lax.broadcasted_iota(jnp.int32, (256, 256), 1)
                value = jnp.where(jnp.logical_or(rows >= cols, i > q), value, 0.0)
                store(a, b, value)

        @pl.when(inner)
        def _():
            update = mm3_t(x_ref[a, 0], y_ref[b, 0])
            update = update + mm3_t(x_ref[a, 1], y_ref[b, 1])
            update = update + mm3_t(x_ref[a, 2], y_ref[b, 2])

            @pl.when(q == missing)
            def _():
                store(a, b, d_ref[n] - update)

            @pl.when(q != missing)
            def _():
                for half in range(2):
                    rows = tile_rows(a, b, half)
                    f_ref[rows, :] = m_ref[rows, :] - update[:, 128 * half : 128 * half + 128]

    for a, b in ((0, 1), (0, 2), (1, 2)):
        store(a, b, jnp.zeros((256, 256), F32))


def call(kernel, outs, ins, specs=None, scratch=(), flops=10**6):
    shapes = [jax.ShapeDtypeStruct(s, F32) for s in outs]
    return pl.pallas_call(
        kernel,
        out_shape=shapes,
        in_specs=specs or [VMEM] * len(ins),
        out_specs=[VMEM] * len(outs),
        scratch_shapes=[pltpu.VMEM(s, F32) for s in scratch],
        compiler_params=PARAMS,
        cost_estimate=pl.CostEstimate(flops=flops, bytes_accessed=4 * 10**6, transcendentals=0),
    )(*ins)


def exchange(x, axis):
    return lax.all_to_all(x, axis, 0, 0, tiled=True)


def shards(matrix, checksum, failed):
    core = lax.axis_index("core")
    p = lax.axis_index(ROW)
    q = lax.axis_index(COL)
    block = matrix.reshape(4608, 128)
    checks = checksum.reshape(3, 256, 3, 256).transpose(0, 2, 1, 3)
    core_arg = core.reshape(1).astype(jnp.int32)

    (col_send,) = call(prepare_kernel, [(16, 104, 256)], [block, failed], [VMEM, SMEM])
    col_got = exchange(col_send, COL)

    top_piece = [jnp.zeros((3, 16, 256), F32)] * PANELS
    for s in range(16):
        target = lax.rem(p + s, 16)
        part = lax.dynamic_slice_in_dim(checks[0], 16 * target, 16, 1)
        if s:
            part = lax.ppermute(part, ROW, [(k, (k + s) % 16) for k in range(PANELS)])
        source = lax.rem(p - s + 16, 16)
        top_piece = [jnp.where(source == k, part, top_piece[k]) for k in range(PANELS)]
    top_piece = jnp.concatenate(top_piece)
    col_got, top_piece = lax.optimization_barrier((col_got, top_piece))

    check_piece = lax.dynamic_slice_in_dim(checks, q * 16, 16, 2)
    panel, lost, lead_send = call(
        rebuild_kernel,
        [(9, 16, 256), (6, 16, 256), (16, 3, 16, 256)],
        [col_got, check_piece],
    )
    row_panel = lax.all_gather(panel, COL)

    top_mine = [top_piece]
    for s in range(1, 8):
        top_mine.append(lax.ppermute(top_piece, "xy", [(i, i ^ s) for i in range(8)]))
    top_mine = jnp.stack(top_mine)
    top_other = lax.ppermute(top_mine, "core", [(0, 1), (1, 0)])

    lead_rows = exchange(lead_send, ROW)
    (half_send,) = call(
        lead_half_kernel, [(16, 6, 8, 256)], [core_arg, lead_rows[:PANELS]], [SMEM, VMEM]
    )
    lead_mine = exchange(half_send, COL)
    lead_other = lax.ppermute(lead_mine, "core", [(0, 1), (1, 0)])

    near = [lost]
    for s in range(1, 8):
        near.append(lax.ppermute(lost, "col_1", [(z, (z + s) % 8) for z in range(8)]))
    near = jnp.stack(near)

    swap = [(i * 16 + j, j * 16 + i) for i in range(16) for j in range(16)]
    col_piece = lax.ppermute(panel, ROW + COL, swap)
    far = lax.ppermute(near, "col_0", [(0, 1), (1, 0)])
    col_piece, lead_mine, far, top_mine = lax.optimization_barrier(
        (col_piece, lead_mine, far, top_mine)
    )
    mine = exchange(jnp.broadcast_to(col_piece[None], (8, *col_piece.shape)), "xy")

    off, inv = call(
        lead_kernel,
        [(PANELS, 256, 256)] * 2,
        [core_arg, lead_mine, lead_other],
        [SMEM, VMEM, VMEM],
        [(6, 256, 256)],
        2 * 10**10,
    )

    mine, inv = lax.optimization_barrier((mine, inv))
    other = lax.ppermute(mine, "core", [(0, 1), (1, 0)])

    missing = col_got[0, 96, 0].astype(jnp.int32)
    place = jnp.stack([p, q, missing]).astype(jnp.int32)
    factored, totals = call(
        finish_kernel,
        [(4608, 128), (3, 3, 256, 256)],
        [place, row_panel, mine, other, top_mine, top_other, near, far, block, checks, off, inv],
        [SMEM] + [VMEM] * 11,
        [(3, 3, 256, 256)] * 3 + [(9, 256, 256)] * 2 + [(6, 256, 256)],
    )
    totals = totals.transpose(0, 2, 1, 3).reshape(checksum.shape)
    return (factored.reshape(matrix.shape), totals)


def solution(mesh):
    finer = Mesh(mesh.devices.reshape(8, 2, 2, 8), ("xy", "core", "col_0", "col_1"))
    in_specs = (P(ROW, None, None, COL, None, None), P(ROW, None, None, None, None), P(COL))
    out_specs = (P(ROW, None, None, COL, None, None), P(ROW, None, None, None, None))
    return jax.shard_map(
        shards, mesh=finer, in_specs=in_specs, out_specs=out_specs, check_vma=False
    )
```

```python
import jax
import jax.numpy as jnp
from jax import lax
from jax.experimental import pallas as pl
from jax.experimental.pallas import tpu as pltpu
from jax.sharding import Mesh
from jax.sharding import PartitionSpec as P

PANELS = 3
ROW = ("xy", "core")
COL = ("col_0", "col_1")
LOWER = [(0, 0), (1, 0), (1, 1), (2, 0), (2, 1), (2, 2)]
F32 = jnp.float32
VMEM = pl.BlockSpec(memory_space=pltpu.VMEM)
SMEM = pl.BlockSpec(memory_space=pltpu.SMEM)


def mm(a, b):
    return lax.dot_general(
        a, b, (((1,), (0,)), ((), ())), precision=lax.Precision.HIGHEST, preferred_element_type=F32
    )


def mm_t(a, b):
    return lax.dot_general(
        a, b, (((1,), (1,)), ((), ())), precision=lax.Precision.HIGHEST, preferred_element_type=F32
    )


def halves(x):
    high = x.astype(jnp.bfloat16)
    return high, (x - high.astype(F32)).astype(jnp.bfloat16)


def high_twice(x, axis):
    high, low = halves(x)
    return jnp.concatenate([high, high, low], axis)


def low_between(x, axis):
    high, low = halves(x)
    return jnp.concatenate([high, low, high], axis)


def dot3(a, b):
    return lax.dot_general(a, b, (((1,), (0,)), ((), ())), preferred_element_type=F32)


def dot3_t(a, b):
    return lax.dot_general(a, b, (((1,), (1,)), ((), ())), preferred_element_type=F32)


def base_inverse(a):
    n = a.shape[0]
    groups = n // 8
    rows = lax.broadcasted_iota(jnp.int32, (8, n), 0)
    lanes = lax.broadcasted_iota(jnp.int32, (8, n), 1)
    ag = [a[8 * g : 8 * g + 8, :] for g in range(groups)]
    mg = [jnp.where(lanes == rows + 8 * g, 1.0, 0.0).astype(F32) for g in range(groups)]
    for m in range(groups):
        columns = [
            [
                jnp.broadcast_to(ag[g][:, 8 * m + k : 8 * m + k + 1], (8, n))
                for g in range(m, groups)
            ]
            for k in range(8)
        ]
        top, mine = ag[m], mg[m]
        us, vs, ls = [], [], []
        for k in range(8):
            scale = lax.rsqrt(columns[k][0][k : k + 1, :])
            l = [x * scale for x in columns[k]]
            for k2 in range(k + 1, 8):
                s = l[0][k2 : k2 + 1, :]
                columns[k2] = [x - y * s for x, y in zip(columns[k2], l)]
            u = top[k : k + 1, :] * scale
            v = mine[k : k + 1, :] * scale
            below = jnp.where(rows > k, l[0], 0.0)
            top = top - below * u
            mine = jnp.where(rows == k, v, mine - below * v)
            us.append(u)
            vs.append(v)
            ls.append(l[1:])
        mg[m] = mine
        for t, g in enumerate(range(m + 1, groups)):
            ag[g] = ag[g] - sum(ls[k][t] * us[k] for k in range(8))
            mg[g] = mg[g] - sum(ls[k][t] * vs[k] for k in range(8))
    return jnp.concatenate(mg, axis=0)


def tile_inverse(a):
    h = a.shape[0] // 2
    first = base_inverse(a[:h, :h])
    l10 = mm_t(a[h:, :h], first)
    second = base_inverse(a[h:, h:] - mm_t(l10, l10))
    low = -mm(second, mm(l10, first))
    return jnp.concatenate(
        [
            jnp.concatenate([first, jnp.zeros_like(first)], 1),
            jnp.concatenate([low, second], 1),
        ],
        0,
    )


def whole(ref, n):
    t = ref[:, n]
    return t.reshape(t.shape[0] * t.shape[1], t.shape[2])


def woven(even, odd, n):
    t = jnp.stack([even[:, n], odd[:, n]], axis=1)
    return t.reshape(256, 256)


def by_core(core, mine_ref, other_ref, body):
    @pl.when(core == 0)
    def _():
        body(mine_ref, other_ref)

    @pl.when(core != 0)
    def _():
        body(other_ref, mine_ref)


def lead_kernel(core_ref, mine_ref, other_ref, off_ref, inv_ref, t_ref):
    def gather(even, odd):
        for n in range(6):
            t_ref[n] = woven(even, odd, n)

    by_core(core_ref[0], mine_ref, other_ref, gather)
    i0 = tile_inverse(t_ref[0])
    inv_ref[0] = i0
    l10 = mm_t(t_ref[1], i0)
    off_ref[0] = l10
    i1 = tile_inverse(t_ref[2] - mm_t(l10, l10))
    inv_ref[1] = i1
    l20 = mm_t(t_ref[3], i0)
    off_ref[1] = l20
    l21 = mm_t(t_ref[4] - mm_t(l20, l10), i1)
    off_ref[2] = l21
    inv_ref[2] = tile_inverse(t_ref[5] - mm_t(l20, l20) - mm_t(l21, l21))


def tile_rows(a, b, half):
    return pl.ds(a * 1536 + 2 * b + half, 256, stride=6)


def prepare_kernel(m_ref, f_ref, col_ref):
    for n, (a, b) in enumerate(LOWER):
        for half in range(2):
            v = m_ref[tile_rows(a, b, half), :].reshape(16, 16, 128)
            col_ref[:, 16 * n : 16 * n + 16, 128 * half : 128 * half + 128] = v
    col_ref[:, 96:104, :] = jnp.full((16, 8, 256), f_ref[0].astype(F32))


def rebuild_kernel(g_ref, c_ref, panel_ref, lost_ref, send_ref):
    missing = g_ref[0, 96:97, :]
    for n, (a, b) in enumerate(LOWER):
        part = slice(16 * n, 16 * n + 16)
        healthy = jnp.zeros((16, 256), F32)
        for j in range(16):
            healthy = healthy + jnp.where(missing != float(j), g_ref[j, part, :], 0.0)
        rebuilt = c_ref[a, b] - healthy
        lost_ref[n] = rebuilt
        if b == 0:
            for k in range(PANELS):
                v = jnp.where(missing == float(k), rebuilt, g_ref[k, part, :])
                panel_ref[3 * a + k] = v
                if a == 0:
                    for s in range(16):
                        send_ref[s, k] = v


def lead_half_kernel(core_ref, g_ref, send_ref):
    rows = pl.ds(pl.multiple_of(8 * core_ref[0], 8), 8)
    for n, (i, k) in enumerate(LOWER):
        v = g_ref[i, k, rows, :]
        for s in range(16):
            send_ref[s, n] = v


def finish_kernel(
    place_ref, r_ref, mine_ref, other_ref, near_ref, far_ref, m_ref, c_ref, off_ref, inv_ref,
    f_ref, t_ref, x_ref, q_ref, k_ref, d_ref, x3_ref, y3_ref, s3_ref, w3_ref,
):
    p, q, missing = place_ref[0], place_ref[1], place_ref[2]

    def gather(even, odd):
        for n in range(9):
            q_ref[n] = woven(even, odd, n)
            k_ref[n] = woven(even, odd, 9 + n)

    by_core(lax.rem(p, 2), mine_ref, other_ref, gather)

    @pl.when(q == missing)
    def _():
        y, z = q // 8, lax.rem(q, 8)
        for s in range(8):
            source = lax.rem(z - s + 8, 8)
            for ref, half in ((near_ref, y), (far_ref, 1 - y)):
                rows = pl.ds(pl.multiple_of(16 * (8 * half + source), 16), 16)
                for n in range(6):
                    d_ref[n, rows, :] = ref[s, n]

    for k in range(PANELS):
        w3_ref[k] = low_between(inv_ref[k], 1)
        w3_ref[3 + k] = low_between(off_ref[k], 1)

    def solve(tile):
        x0 = dot3_t(high_twice(tile(0), 1), w3_ref[0])
        x0_3 = high_twice(x0, 1)
        x1 = dot3_t(high_twice(tile(1) - dot3_t(x0_3, w3_ref[3]), 1), w3_ref[1])
        x1_3 = high_twice(x1, 1)
        rest = tile(2) - dot3_t(x0_3, w3_ref[4]) - dot3_t(x1_3, w3_ref[5])
        x2 = dot3_t(high_twice(rest, 1), w3_ref[2])
        return (x0, x1, x2), (x0_3, x1_3)

    @pl.loop(0, 3)
    def _(a):
        xs, (x0_3, x1_3) = solve(lambda k: whole(r_ref, 3 * a + k))
        for k in range(PANELS):
            x_ref[a, k] = xs[k]
        x3_ref[a, :, 0:768] = x0_3
        x3_ref[a, :, 768:1536] = x1_3
        x3_ref[a, :, 1536:2304] = high_twice(xs[2], 1)

    @pl.loop(0, 3)
    def _(b):
        ys, _ = solve(lambda k: q_ref[3 * b + k])
        for k in range(PANELS):
            y3_ref[b, :, 768 * k : 768 * k + 768] = low_between(ys[k], 1)

    @pl.loop(0, 3)
    def _(b):
        s0 = dot3(w3_ref[0], high_twice(k_ref[b], 0))
        s3_ref[b, 0:768] = low_between(s0, 0)
        s0_3 = high_twice(s0, 0)
        s1 = dot3(w3_ref[1], high_twice(k_ref[3 + b] - dot3(w3_ref[3], s0_3), 0))
        s3_ref[b, 768:1536] = low_between(s1, 0)
        s1_3 = high_twice(s1, 0)
        rest = k_ref[6 + b] - dot3(w3_ref[4], s0_3) - dot3(w3_ref[5], s1_3)
        s2 = dot3(w3_ref[2], high_twice(rest, 0))
        s3_ref[b, 1536:2304] = low_between(s2, 0)

    @pl.loop(0, 9)
    def _(n):
        a, b = n // 3, n % 3
        t_ref[a, b] = c_ref[a, b] - dot3(x3_ref[a], s3_ref[b])

    def store(a, b, value):
        for half in range(2):
            f_ref[tile_rows(a, b, half), :] = value[:, 128 * half : 128 * half + 128]

    for n, (a, b) in enumerate(LOWER):
        i, j = p + 16 * a, q + 16 * b
        kept = i >= j
        panel = jnp.logical_and(kept, j < PANELS) if b == 0 else jnp.bool_(False)
        inner = jnp.logical_and(kept, jnp.logical_not(panel))

        @pl.when(jnp.logical_not(kept))
        def _():
            store(a, b, jnp.zeros((256, 256), F32))

        if b == 0:

            @pl.when(panel)
            def _():
                value = x_ref[a, jnp.minimum(q, PANELS - 1)]
                rows = lax.broadcasted_iota(jnp.int32, (256, 256), 0)
                cols = lax.broadcasted_iota(jnp.int32, (256, 256), 1)
                value = jnp.where(jnp.logical_or(rows >= cols, i > q), value, 0.0)
                store(a, b, value)

        @pl.when(inner)
        def _():
            update = dot3_t(x3_ref[a], y3_ref[b])

            @pl.when(q == missing)
            def _():
                store(a, b, d_ref[n] - update)

            @pl.when(q != missing)
            def _():
                for half in range(2):
                    rows = tile_rows(a, b, half)
                    f_ref[rows, :] = m_ref[rows, :] - update[:, 128 * half : 128 * half + 128]

    for a, b in ((0, 1), (0, 2), (1, 2)):
        store(a, b, jnp.zeros((256, 256), F32))


def call(
    kernel, outs, ins, specs=None, scratch=(), flops=10**6, halves_scratch=(), limit=16
):
    shapes = [jax.ShapeDtypeStruct(s, F32) for s in outs]
    return pl.pallas_call(
        kernel,
        out_shape=shapes,
        in_specs=specs or [VMEM] * len(ins),
        out_specs=[VMEM] * len(outs),
        scratch_shapes=[pltpu.VMEM(s, F32) for s in scratch]
        + [pltpu.VMEM(s, jnp.bfloat16) for s in halves_scratch],
        compiler_params=pltpu.CompilerParams(vmem_limit_bytes=limit << 20),
        cost_estimate=pl.CostEstimate(flops=flops, bytes_accessed=4 * 10**6, transcendentals=0),
    )(*ins)


def exchange(x, axis):
    return lax.all_to_all(x, axis, 0, 0, tiled=True)


def shards(matrix, checksum, failed):
    core = lax.axis_index("core")
    p = lax.axis_index(ROW)
    q = lax.axis_index(COL)
    block = matrix.reshape(4608, 128)
    checks = checksum.reshape(3, 256, 3, 256).transpose(0, 2, 1, 3)
    core_arg = core.reshape(1).astype(jnp.int32)

    (col_send,) = call(prepare_kernel, [(16, 104, 256)], [block, failed], [VMEM, SMEM])
    col_got = exchange(col_send, COL)

    top_piece = [jnp.zeros((3, 16, 256), F32)] * PANELS
    for s in range(16):
        target = lax.rem(p + s, 16)
        part = lax.dynamic_slice_in_dim(checks[0], 16 * target, 16, 1)
        if s:
            part = lax.ppermute(part, ROW, [(k, (k + s) % 16) for k in range(PANELS)])
        source = lax.rem(p - s + 16, 16)
        top_piece = [jnp.where(source == k, part, top_piece[k]) for k in range(PANELS)]
    top_piece = jnp.concatenate(top_piece)
    col_got, top_piece = lax.optimization_barrier((col_got, top_piece))

    check_piece = lax.dynamic_slice_in_dim(checks, q * 16, 16, 2)
    panel, lost, lead_send = call(
        rebuild_kernel,
        [(9, 16, 256), (6, 16, 256), (16, 3, 16, 256)],
        [col_got, check_piece],
    )
    row_panel = lax.all_gather(panel, COL)

    swap = [(i * 16 + j, j * 16 + i) for i in range(16) for j in range(16)]
    col_piece = lax.ppermute(panel, ROW + COL, swap)
    lead_rows = exchange(lead_send, ROW)
    lead_rows, col_piece = lax.optimization_barrier((lead_rows, col_piece))
    (half_send,) = call(
        lead_half_kernel, [(16, 6, 8, 256)], [core_arg, lead_rows[:PANELS]], [SMEM, VMEM]
    )
    lead_mine = exchange(half_send, COL)
    lead_other = lax.ppermute(lead_mine, "core", [(0, 1), (1, 0)])

    near = [lost]
    for s in range(1, 8):
        near.append(lax.ppermute(lost, "col_1", [(z, (z + s) % 8) for z in range(8)]))
    near = jnp.stack(near)

    far = lax.ppermute(near, "col_0", [(0, 1), (1, 0)])
    both = jnp.concatenate([col_piece, top_piece])
    both, lead_mine, far, row_panel = lax.optimization_barrier((both, lead_mine, far, row_panel))
    mine = exchange(jnp.broadcast_to(both[None], (8, *both.shape)), "xy")

    off, inv = call(
        lead_kernel,
        [(PANELS, 256, 256)] * 2,
        [core_arg, lead_mine, lead_other],
        [SMEM, VMEM, VMEM],
        [(6, 256, 256)],
        2 * 10**10,
    )

    mine, inv = lax.optimization_barrier((mine, inv))
    other = lax.ppermute(mine, "core", [(0, 1), (1, 0)])

    missing = col_got[0, 96, 0].astype(jnp.int32)
    place = jnp.stack([p, q, missing]).astype(jnp.int32)
    factored, totals = call(
        finish_kernel,
        [(4608, 128), (3, 3, 256, 256)],
        [place, row_panel, mine, other, near, far, block, checks, off, inv],
        [SMEM] + [VMEM] * 9,
        [(3, 3, 256, 256)] + [(9, 256, 256)] * 2 + [(6, 256, 256)],
        halves_scratch=[(3, 256, 2304)] * 2 + [(3, 2304, 256), (6, 256, 768)],
        limit=40,
    )
    totals = totals.transpose(0, 2, 1, 3).reshape(checksum.shape)
    return (factored.reshape(matrix.shape), totals)


def solution(mesh):
    finer = Mesh(mesh.devices.reshape(8, 2, 2, 8), ("xy", "core", "col_0", "col_1"))
    in_specs = (P(ROW, None, None, COL, None, None), P(ROW, None, None, None, None), P(COL))
    out_specs = (P(ROW, None, None, COL, None, None), P(ROW, None, None, None, None))
    return jax.shard_map(
        shards, mesh=finer, in_specs=in_specs, out_specs=out_specs, check_vma=False
    )
```

```python
import jax
import jax.numpy as jnp
from jax import lax
from jax.experimental import pallas as pl
from jax.experimental.pallas import tpu as pltpu
from jax.sharding import Mesh
from jax.sharding import PartitionSpec as P

PANELS = 3
ROW = ("xy", "core")
COL = ("col_0", "col_1")
LOWER = [(0, 0), (1, 0), (1, 1), (2, 0), (2, 1), (2, 2)]
F32 = jnp.float32
VMEM = pl.BlockSpec(memory_space=pltpu.VMEM)
SMEM = pl.BlockSpec(memory_space=pltpu.SMEM)


def mm(a, b):
    return lax.dot_general(
        a, b, (((1,), (0,)), ((), ())), precision=lax.Precision.HIGHEST, preferred_element_type=F32
    )


def mm_t(a, b):
    return lax.dot_general(
        a, b, (((1,), (1,)), ((), ())), precision=lax.Precision.HIGHEST, preferred_element_type=F32
    )


def halves(x):
    high = x.astype(jnp.bfloat16)
    return high, (x - high.astype(F32)).astype(jnp.bfloat16)


def high_twice(x, axis):
    high, low = halves(x)
    return jnp.concatenate([high, high, low], axis)


def low_between(x, axis):
    high, low = halves(x)
    return jnp.concatenate([high, low, high], axis)


def dot3(a, b):
    return lax.dot_general(a, b, (((1,), (0,)), ((), ())), preferred_element_type=F32)


def dot3_t(a, b):
    return lax.dot_general(a, b, (((1,), (1,)), ((), ())), preferred_element_type=F32)


def base_inverse(a):
    n = a.shape[0]
    groups = n // 8
    rows = lax.broadcasted_iota(jnp.int32, (8, n), 0)
    lanes = lax.broadcasted_iota(jnp.int32, (8, n), 1)
    ag = [a[8 * g : 8 * g + 8, :] for g in range(groups)]
    mg = [jnp.where(lanes == rows + 8 * g, 1.0, 0.0).astype(F32) for g in range(groups)]
    for m in range(groups):
        columns = [
            [
                jnp.broadcast_to(ag[g][:, 8 * m + k : 8 * m + k + 1], (8, n))
                for g in range(m, groups)
            ]
            for k in range(8)
        ]
        top, mine = ag[m], mg[m]
        us, vs, ls = [], [], []
        for k in range(8):
            scale = lax.rsqrt(columns[k][0][k : k + 1, :])
            l = [x * scale for x in columns[k]]
            for k2 in range(k + 1, 8):
                s = l[0][k2 : k2 + 1, :]
                columns[k2] = [x - y * s for x, y in zip(columns[k2], l)]
            u = top[k : k + 1, :] * scale
            v = mine[k : k + 1, :] * scale
            below = jnp.where(rows > k, l[0], 0.0)
            top = top - below * u
            mine = jnp.where(rows == k, v, mine - below * v)
            us.append(u)
            vs.append(v)
            ls.append(l[1:])
        mg[m] = mine
        for t, g in enumerate(range(m + 1, groups)):
            ag[g] = ag[g] - sum(ls[k][t] * us[k] for k in range(8))
            mg[g] = mg[g] - sum(ls[k][t] * vs[k] for k in range(8))
    return jnp.concatenate(mg, axis=0)


def tile_inverse(a):
    h = a.shape[0] // 2
    first = base_inverse(a[:h, :h])
    l10 = mm_t(a[h:, :h], first)
    second = base_inverse(a[h:, h:] - mm_t(l10, l10))
    low = -mm(second, mm(l10, first))
    return jnp.concatenate(
        [
            jnp.concatenate([first, jnp.zeros_like(first)], 1),
            jnp.concatenate([low, second], 1),
        ],
        0,
    )


def whole(ref, n):
    t = ref[:, n]
    return t.reshape(t.shape[0] * t.shape[1], t.shape[2])


def woven(even, odd, n):
    t = jnp.stack([even[:, n], odd[:, n]], axis=1)
    return t.reshape(256, 256)


def by_core(core, mine_ref, other_ref, body):
    @pl.when(core == 0)
    def _():
        body(mine_ref, other_ref)

    @pl.when(core != 0)
    def _():
        body(other_ref, mine_ref)


def lead_kernel(core_ref, mine_ref, other_ref, off_ref, inv_ref, t_ref):
    def gather(even, odd):
        for n in range(6):
            t_ref[n] = woven(even, odd, n)

    by_core(core_ref[0], mine_ref, other_ref, gather)
    i0 = tile_inverse(t_ref[0])
    inv_ref[0] = i0
    l10 = mm_t(t_ref[1], i0)
    off_ref[0] = l10
    i1 = tile_inverse(t_ref[2] - mm_t(l10, l10))
    inv_ref[1] = i1
    l20 = mm_t(t_ref[3], i0)
    off_ref[1] = l20
    l21 = mm_t(t_ref[4] - mm_t(l20, l10), i1)
    off_ref[2] = l21
    inv_ref[2] = tile_inverse(t_ref[5] - mm_t(l20, l20) - mm_t(l21, l21))


def tile_rows(a, b, half):
    return pl.ds(a * 1536 + 2 * b + half, 256, stride=6)


def prepare_kernel(m_ref, f_ref, col_ref):
    for n, (a, b) in enumerate(LOWER):
        for half in range(2):
            v = m_ref[tile_rows(a, b, half), :].reshape(16, 16, 128)
            col_ref[:, 16 * n : 16 * n + 16, 128 * half : 128 * half + 128] = v
    col_ref[:, 96:104, :] = jnp.full((16, 8, 256), f_ref[0].astype(F32))


def rebuild_kernel(g_ref, c_ref, panel_ref, lost_ref, send_ref):
    missing = g_ref[0, 96:97, :]
    for n, (a, b) in enumerate(LOWER):
        part = slice(16 * n, 16 * n + 16)
        healthy = jnp.zeros((16, 256), F32)
        for j in range(16):
            healthy = healthy + jnp.where(missing != float(j), g_ref[j, part, :], 0.0)
        rebuilt = c_ref[a, b] - healthy
        lost_ref[n] = rebuilt
        if b == 0:
            for k in range(PANELS):
                v = jnp.where(missing == float(k), rebuilt, g_ref[k, part, :])
                panel_ref[3 * a + k] = v
                if a == 0:
                    for s in range(16):
                        send_ref[s, k] = v


def lead_half_kernel(core_ref, g_ref, send_ref):
    rows = pl.ds(pl.multiple_of(8 * core_ref[0], 8), 8)
    for n, (i, k) in enumerate(LOWER):
        v = g_ref[i, k, rows, :]
        for s in range(16):
            send_ref[s, n] = v


def solve_kernel(
    core_ref, r_ref, mine_ref, other_ref, c_ref, off_ref, inv_ref,
    t_ref, x_ref, x3_ref, y3_ref, q_ref, k_ref, s3_ref, w3_ref,
):

    def gather(even, odd):
        for n in range(9):
            q_ref[n] = woven(even, odd, n)
            k_ref[n] = woven(even, odd, 9 + n)

    by_core(core_ref[0], mine_ref, other_ref, gather)

    for k in range(PANELS):
        w3_ref[k] = low_between(inv_ref[k], 1)
        w3_ref[3 + k] = low_between(off_ref[k], 1)

    def solve(tile):
        x0 = dot3_t(high_twice(tile(0), 1), w3_ref[0])
        x0_3 = high_twice(x0, 1)
        x1 = dot3_t(high_twice(tile(1) - dot3_t(x0_3, w3_ref[3]), 1), w3_ref[1])
        x1_3 = high_twice(x1, 1)
        rest = tile(2) - dot3_t(x0_3, w3_ref[4]) - dot3_t(x1_3, w3_ref[5])
        x2 = dot3_t(high_twice(rest, 1), w3_ref[2])
        return (x0, x1, x2), (x0_3, x1_3)

    @pl.loop(0, 3)
    def _(a):
        xs, (x0_3, x1_3) = solve(lambda k: whole(r_ref, 3 * a + k))
        for k in range(PANELS):
            x_ref[a, k] = xs[k]
        x3_ref[a, :, 0:768] = x0_3
        x3_ref[a, :, 768:1536] = x1_3
        x3_ref[a, :, 1536:2304] = high_twice(xs[2], 1)

    @pl.loop(0, 3)
    def _(b):
        ys, _ = solve(lambda k: q_ref[3 * b + k])
        for k in range(PANELS):
            y3_ref[b, :, 768 * k : 768 * k + 768] = low_between(ys[k], 1)

    @pl.loop(0, 3)
    def _(b):
        s0 = dot3(w3_ref[0], high_twice(k_ref[b], 0))
        s3_ref[b, 0:768] = low_between(s0, 0)
        s0_3 = high_twice(s0, 0)
        s1 = dot3(w3_ref[1], high_twice(k_ref[3 + b] - dot3(w3_ref[3], s0_3), 0))
        s3_ref[b, 768:1536] = low_between(s1, 0)
        s1_3 = high_twice(s1, 0)
        rest = k_ref[6 + b] - dot3(w3_ref[4], s0_3) - dot3(w3_ref[5], s1_3)
        s2 = dot3(w3_ref[2], high_twice(rest, 0))
        s3_ref[b, 1536:2304] = low_between(s2, 0)

    @pl.loop(0, 9)
    def _(n):
        a, b = n // 3, n % 3
        t_ref[a, b] = c_ref[a, b] - dot3(x3_ref[a], s3_ref[b])


def finish_kernel(place_ref, d_ref, m_ref, x_ref, x3_ref, y3_ref, f_ref):
    p, q, missing = place_ref[0], place_ref[1], place_ref[2]

    def store(a, b, value):
        for half in range(2):
            f_ref[tile_rows(a, b, half), :] = value[:, 128 * half : 128 * half + 128]

    for n, (a, b) in enumerate(LOWER):
        i, j = p + 16 * a, q + 16 * b
        kept = i >= j
        panel = jnp.logical_and(kept, j < PANELS) if b == 0 else jnp.bool_(False)
        inner = jnp.logical_and(kept, jnp.logical_not(panel))

        @pl.when(jnp.logical_not(kept))
        def _():
            store(a, b, jnp.zeros((256, 256), F32))

        if b == 0:

            @pl.when(panel)
            def _():
                value = x_ref[a, jnp.minimum(q, PANELS - 1)]
                rows = lax.broadcasted_iota(jnp.int32, (256, 256), 0)
                cols = lax.broadcasted_iota(jnp.int32, (256, 256), 1)
                value = jnp.where(jnp.logical_or(rows >= cols, i > q), value, 0.0)
                store(a, b, value)

        @pl.when(inner)
        def _():
            update = dot3_t(x3_ref[a], y3_ref[b])

            @pl.when(q == missing)
            def _():
                store(a, b, whole(d_ref, n) - update)

            @pl.when(q != missing)
            def _():
                for half in range(2):
                    rows = tile_rows(a, b, half)
                    f_ref[rows, :] = m_ref[rows, :] - update[:, 128 * half : 128 * half + 128]

    for a, b in ((0, 1), (0, 2), (1, 2)):
        store(a, b, jnp.zeros((256, 256), F32))


def call(
    kernel, outs, ins, specs=None, scratch=(), flops=10**6,
    halves_outs=(), halves_scratch=(), limit=16,
):
    shapes = [jax.ShapeDtypeStruct(s, F32) for s in outs]
    shapes += [jax.ShapeDtypeStruct(s, jnp.bfloat16) for s in halves_outs]
    return pl.pallas_call(
        kernel,
        out_shape=shapes,
        in_specs=specs or [VMEM] * len(ins),
        out_specs=[VMEM] * len(shapes),
        scratch_shapes=[pltpu.VMEM(s, F32) for s in scratch]
        + [pltpu.VMEM(s, jnp.bfloat16) for s in halves_scratch],
        compiler_params=pltpu.CompilerParams(vmem_limit_bytes=limit << 20),
        cost_estimate=pl.CostEstimate(flops=flops, bytes_accessed=4 * 10**6, transcendentals=0),
    )(*ins)


def exchange(x, axis):
    return lax.all_to_all(x, axis, 0, 0, tiled=True)


def shards(matrix, checksum, failed):
    core = lax.axis_index("core")
    p = lax.axis_index(ROW)
    q = lax.axis_index(COL)
    block = matrix.reshape(4608, 128)
    checks = checksum.reshape(3, 256, 3, 256).transpose(0, 2, 1, 3)
    core_arg = core.reshape(1).astype(jnp.int32)

    (col_send,) = call(prepare_kernel, [(16, 104, 256)], [block, failed], [VMEM, SMEM])
    col_got = exchange(col_send, COL)

    top_piece = [jnp.zeros((3, 16, 256), F32)] * PANELS
    for s in range(16):
        target = lax.rem(p + s, 16)
        part = lax.dynamic_slice_in_dim(checks[0], 16 * target, 16, 1)
        if s:
            part = lax.ppermute(part, ROW, [(k, (k + s) % 16) for k in range(PANELS)])
        source = lax.rem(p - s + 16, 16)
        top_piece = [jnp.where(source == k, part, top_piece[k]) for k in range(PANELS)]
    top_piece = jnp.concatenate(top_piece)
    col_got, top_piece = lax.optimization_barrier((col_got, top_piece))

    check_piece = lax.dynamic_slice_in_dim(checks, q * 16, 16, 2)
    panel, lost, lead_send = call(
        rebuild_kernel,
        [(9, 16, 256), (6, 16, 256), (16, 3, 16, 256)],
        [col_got, check_piece],
    )
    row_panel = lax.all_gather(panel, COL)
    lost_all = lax.all_gather(lost, COL)

    swap = [(i * 16 + j, j * 16 + i) for i in range(16) for j in range(16)]
    col_piece = lax.ppermute(panel, ROW + COL, swap)
    lead_rows = exchange(lead_send, ROW)
    lead_rows, col_piece = lax.optimization_barrier((lead_rows, col_piece))
    (half_send,) = call(
        lead_half_kernel, [(16, 6, 8, 256)], [core_arg, lead_rows[:PANELS]], [SMEM, VMEM]
    )
    lead_mine = exchange(half_send, COL)
    lead_other = lax.ppermute(lead_mine, "core", [(0, 1), (1, 0)])

    both = jnp.concatenate([col_piece, top_piece])
    both, lead_mine, row_panel = lax.optimization_barrier((both, lead_mine, row_panel))
    mine = exchange(jnp.broadcast_to(both[None], (8, *both.shape)), "xy")

    off, inv = call(
        lead_kernel,
        [(PANELS, 256, 256)] * 2,
        [core_arg, lead_mine, lead_other],
        [SMEM, VMEM, VMEM],
        [(6, 256, 256)],
        2 * 10**10,
    )

    mine, inv = lax.optimization_barrier((mine, inv))
    other = lax.ppermute(mine, "core", [(0, 1), (1, 0)])

    totals, x, x3, y3 = call(
        solve_kernel,
        [(3, 3, 256, 256)] * 2,
        [core_arg, row_panel, mine, other, checks, off, inv],
        [SMEM] + [VMEM] * 6,
        [(9, 256, 256)] * 2,
        3 * 10**9,
        halves_outs=[(3, 256, 2304)] * 2,
        halves_scratch=[(3, 2304, 256), (6, 256, 768)],
        limit=32,
    )

    missing = col_got[0, 96, 0].astype(jnp.int32)
    place = jnp.stack([p, q, missing]).astype(jnp.int32)
    (factored,) = call(
        finish_kernel,
        [(4608, 128)],
        [place, lost_all, block, x, x3, y3],
        [SMEM] + [VMEM] * 5,
    )
    totals = totals.transpose(0, 2, 1, 3).reshape(checksum.shape)
    return (factored.reshape(matrix.shape), totals)


def solution(mesh):
    finer = Mesh(mesh.devices.reshape(8, 2, 2, 8), ("xy", "core", "col_0", "col_1"))
    in_specs = (P(ROW, None, None, COL, None, None), P(ROW, None, None, None, None), P(COL))
    out_specs = (P(ROW, None, None, COL, None, None), P(ROW, None, None, None, None))
    return jax.shard_map(
        shards, mesh=finer, in_specs=in_specs, out_specs=out_specs, check_vma=False
    )
```

```python
import jax
import jax.numpy as jnp
from jax import lax
from jax.experimental import pallas as pl
from jax.experimental.pallas import tpu as pltpu
from jax.sharding import Mesh
from jax.sharding import PartitionSpec as P

PANELS = 3
ROW = ("xy", "core")
COL = ("col_0", "col_1")
LOWER = [(0, 0), (1, 0), (1, 1), (2, 0), (2, 1), (2, 2)]
F32 = jnp.float32
VMEM = pl.BlockSpec(memory_space=pltpu.VMEM)
SMEM = pl.BlockSpec(memory_space=pltpu.SMEM)


def mm(a, b):
    return lax.dot_general(
        a, b, (((1,), (0,)), ((), ())), precision=lax.Precision.HIGHEST, preferred_element_type=F32
    )


def mm_t(a, b):
    return lax.dot_general(
        a, b, (((1,), (1,)), ((), ())), precision=lax.Precision.HIGHEST, preferred_element_type=F32
    )


def halves(x):
    high = x.astype(jnp.bfloat16)
    return high, (x - high.astype(F32)).astype(jnp.bfloat16)


def high_twice(x, axis):
    high, low = halves(x)
    return jnp.concatenate([high, high, low], axis)


def low_between(x, axis):
    high, low = halves(x)
    return jnp.concatenate([high, low, high], axis)


def dot3(a, b):
    return lax.dot_general(a, b, (((1,), (0,)), ((), ())), preferred_element_type=F32)


def dot3_t(a, b):
    return lax.dot_general(a, b, (((1,), (1,)), ((), ())), preferred_element_type=F32)


def base_inverse(a):
    n = a.shape[0]
    groups = n // 8
    rows = lax.broadcasted_iota(jnp.int32, (8, n), 0)
    lanes = lax.broadcasted_iota(jnp.int32, (8, n), 1)
    ag = [a[8 * g : 8 * g + 8, :] for g in range(groups)]
    mg = [jnp.where(lanes == rows + 8 * g, 1.0, 0.0).astype(F32) for g in range(groups)]
    for m in range(groups):
        columns = [
            [
                jnp.broadcast_to(ag[g][:, 8 * m + k : 8 * m + k + 1], (8, n))
                for g in range(m, groups)
            ]
            for k in range(8)
        ]
        top, mine = ag[m], mg[m]
        us, vs, ls = [], [], []
        for k in range(8):
            scale = lax.rsqrt(columns[k][0][k : k + 1, :])
            l = [x * scale for x in columns[k]]
            for k2 in range(k + 1, 8):
                s = l[0][k2 : k2 + 1, :]
                columns[k2] = [x - y * s for x, y in zip(columns[k2], l)]
            u = top[k : k + 1, :] * scale
            v = mine[k : k + 1, :] * scale
            below = jnp.where(rows > k, l[0], 0.0)
            top = top - below * u
            mine = jnp.where(rows == k, v, mine - below * v)
            us.append(u)
            vs.append(v)
            ls.append(l[1:])
        mg[m] = mine
        for t, g in enumerate(range(m + 1, groups)):
            ag[g] = ag[g] - sum(ls[k][t] * us[k] for k in range(8))
            mg[g] = mg[g] - sum(ls[k][t] * vs[k] for k in range(8))
    return jnp.concatenate(mg, axis=0)


def tile_inverse(a):
    h = a.shape[0] // 2
    first = base_inverse(a[:h, :h])
    l10 = mm_t(a[h:, :h], first)
    second = base_inverse(a[h:, h:] - mm_t(l10, l10))
    low = -mm(second, mm(l10, first))
    return jnp.concatenate(
        [
            jnp.concatenate([first, jnp.zeros_like(first)], 1),
            jnp.concatenate([low, second], 1),
        ],
        0,
    )


def whole(ref, n):
    t = ref[:, n]
    return t.reshape(t.shape[0] * t.shape[1], t.shape[2])


def woven(even, odd, n):
    t = jnp.stack([even[:, n], odd[:, n]], axis=1)
    return t.reshape(256, 256)


def by_core(core, mine_ref, other_ref, body):
    @pl.when(core == 0)
    def _():
        body(mine_ref, other_ref)

    @pl.when(core != 0)
    def _():
        body(other_ref, mine_ref)


def lead_kernel(core_ref, mine_ref, other_ref, off_ref, inv_ref, t_ref):
    def gather(even, odd):
        for n in range(6):
            t_ref[n] = woven(even, odd, n)

    by_core(core_ref[0], mine_ref, other_ref, gather)
    i0 = tile_inverse(t_ref[0])
    inv_ref[0] = i0
    l10 = mm_t(t_ref[1], i0)
    off_ref[0] = l10
    i1 = tile_inverse(t_ref[2] - mm_t(l10, l10))
    inv_ref[1] = i1
    l20 = mm_t(t_ref[3], i0)
    off_ref[1] = l20
    l21 = mm_t(t_ref[4] - mm_t(l20, l10), i1)
    off_ref[2] = l21
    inv_ref[2] = tile_inverse(t_ref[5] - mm_t(l20, l20) - mm_t(l21, l21))


def tile_rows(a, b, half):
    return pl.ds(a * 1536 + 2 * b + half, 256, stride=6)


def prepare_kernel(m_ref, f_ref, col_ref):
    for n, (a, b) in enumerate(LOWER):
        for half in range(2):
            v = m_ref[tile_rows(a, b, half), :].reshape(16, 16, 128)
            col_ref[:, 16 * n : 16 * n + 16, 128 * half : 128 * half + 128] = v
    col_ref[:, 96:104, :] = jnp.full((16, 8, 256), f_ref[0].astype(F32))


def rebuild_kernel(g_ref, c_ref, panel_ref, lost_ref, send_ref):
    missing = g_ref[0, 96:97, :]
    for n, (a, b) in enumerate(LOWER):
        part = slice(16 * n, 16 * n + 16)
        healthy = jnp.zeros((16, 256), F32)
        for j in range(16):
            healthy = healthy + jnp.where(missing != float(j), g_ref[j, part, :], 0.0)
        rebuilt = c_ref[a, b] - healthy
        lost_ref[n] = rebuilt
        if b == 0:
            for k in range(PANELS):
                v = jnp.where(missing == float(k), rebuilt, g_ref[k, part, :])
                panel_ref[3 * a + k] = v
                if a == 0:
                    for s in range(16):
                        send_ref[s, k] = v


def lead_half_kernel(core_ref, g_ref, send_ref):
    rows = pl.ds(pl.multiple_of(8 * core_ref[0], 8), 8)
    for n, (i, k) in enumerate(LOWER):
        v = g_ref[i, k, rows, :]
        for s in range(16):
            send_ref[s, n] = v


def solve_kernel(
    core_ref, r_ref, mine_ref, other_ref, c_ref, off_ref, inv_ref,
    t_ref, x3_ref, y3_ref, q_ref, k_ref, s3_ref, w3_ref,
):

    def gather(even, odd):
        for n in range(9):
            q_ref[n] = woven(even, odd, n)
            k_ref[n] = woven(even, odd, 9 + n)

    by_core(core_ref[0], mine_ref, other_ref, gather)

    for k in range(PANELS):
        w3_ref[k] = low_between(inv_ref[k], 1)
        w3_ref[3 + k] = low_between(off_ref[k], 1)

    def solve(tile):
        x0 = dot3_t(high_twice(tile(0), 1), w3_ref[0])
        x0_3 = high_twice(x0, 1)
        x1 = dot3_t(high_twice(tile(1) - dot3_t(x0_3, w3_ref[3]), 1), w3_ref[1])
        x1_3 = high_twice(x1, 1)
        rest = tile(2) - dot3_t(x0_3, w3_ref[4]) - dot3_t(x1_3, w3_ref[5])
        x2 = dot3_t(high_twice(rest, 1), w3_ref[2])
        return (x0, x1, x2), (x0_3, x1_3)

    @pl.loop(0, 3)
    def _(a):
        xs, (x0_3, x1_3) = solve(lambda k: whole(r_ref, 3 * a + k))
        x3_ref[a, :, 0:768] = x0_3
        x3_ref[a, :, 768:1536] = x1_3
        x3_ref[a, :, 1536:2304] = high_twice(xs[2], 1)

    @pl.loop(0, 3)
    def _(b):
        ys, _ = solve(lambda k: q_ref[3 * b + k])
        for k in range(PANELS):
            y3_ref[b, :, 768 * k : 768 * k + 768] = low_between(ys[k], 1)

    @pl.loop(0, 3)
    def _(b):
        s0 = dot3(w3_ref[0], high_twice(k_ref[b], 0))
        s3_ref[b, 0:768] = low_between(s0, 0)
        s0_3 = high_twice(s0, 0)
        s1 = dot3(w3_ref[1], high_twice(k_ref[3 + b] - dot3(w3_ref[3], s0_3), 0))
        s3_ref[b, 768:1536] = low_between(s1, 0)
        s1_3 = high_twice(s1, 0)
        rest = k_ref[6 + b] - dot3(w3_ref[4], s0_3) - dot3(w3_ref[5], s1_3)
        s2 = dot3(w3_ref[2], high_twice(rest, 0))
        s3_ref[b, 1536:2304] = low_between(s2, 0)

    @pl.loop(0, 9)
    def _(n):
        a, b = n // 3, n % 3
        t_ref[a, b] = c_ref[a, b] - dot3(x3_ref[a], s3_ref[b])


def finish_kernel(place_ref, d_ref, m_ref, x3_ref, y3_ref, f_ref):
    p, q, missing = place_ref[0], place_ref[1], place_ref[2]

    def store(a, b, value):
        for half in range(2):
            f_ref[tile_rows(a, b, half), :] = value[:, 128 * half : 128 * half + 128]

    for n, (a, b) in enumerate(LOWER):
        i, j = p + 16 * a, q + 16 * b
        kept = i >= j
        panel = jnp.logical_and(kept, j < PANELS) if b == 0 else jnp.bool_(False)
        inner = jnp.logical_and(kept, jnp.logical_not(panel))

        @pl.when(jnp.logical_not(kept))
        def _():
            store(a, b, jnp.zeros((256, 256), F32))

        if b == 0:

            @pl.when(panel)
            def _():
                start = pl.multiple_of(768 * jnp.minimum(q, PANELS - 1), 128)
                value = x3_ref[a, :, pl.ds(start, 256)].astype(F32)
                value = value + x3_ref[a, :, pl.ds(start + 512, 256)].astype(F32)
                rows = lax.broadcasted_iota(jnp.int32, (256, 256), 0)
                cols = lax.broadcasted_iota(jnp.int32, (256, 256), 1)
                value = jnp.where(jnp.logical_or(rows >= cols, i > q), value, 0.0)
                store(a, b, value)

        @pl.when(inner)
        def _():
            update = dot3_t(x3_ref[a], y3_ref[b])

            @pl.when(q == missing)
            def _():
                store(a, b, whole(d_ref, n) - update)

            @pl.when(q != missing)
            def _():
                for half in range(2):
                    rows = tile_rows(a, b, half)
                    f_ref[rows, :] = m_ref[rows, :] - update[:, 128 * half : 128 * half + 128]

    for a, b in ((0, 1), (0, 2), (1, 2)):
        store(a, b, jnp.zeros((256, 256), F32))


def call(
    kernel, outs, ins, specs=None, scratch=(), flops=10**6,
    halves_outs=(), halves_scratch=(), limit=16,
):
    shapes = [jax.ShapeDtypeStruct(s, F32) for s in outs]
    shapes += [jax.ShapeDtypeStruct(s, jnp.bfloat16) for s in halves_outs]
    return pl.pallas_call(
        kernel,
        out_shape=shapes,
        in_specs=specs or [VMEM] * len(ins),
        out_specs=[VMEM] * len(shapes),
        scratch_shapes=[pltpu.VMEM(s, F32) for s in scratch]
        + [pltpu.VMEM(s, jnp.bfloat16) for s in halves_scratch],
        compiler_params=pltpu.CompilerParams(vmem_limit_bytes=limit << 20),
        cost_estimate=pl.CostEstimate(flops=flops, bytes_accessed=4 * 10**6, transcendentals=0),
    )(*ins)


def exchange(x, axis):
    return lax.all_to_all(x, axis, 0, 0, tiled=True)


def shards(matrix, checksum, failed):
    core = lax.axis_index("core")
    p = lax.axis_index(ROW)
    q = lax.axis_index(COL)
    block = matrix.reshape(4608, 128)
    checks = checksum.reshape(3, 256, 3, 256).transpose(0, 2, 1, 3)
    core_arg = core.reshape(1).astype(jnp.int32)

    (col_send,) = call(prepare_kernel, [(16, 104, 256)], [block, failed], [VMEM, SMEM])
    col_got = exchange(col_send, COL)

    top_piece = [jnp.zeros((3, 16, 256), F32)] * PANELS
    for s in range(16):
        target = lax.rem(p + s, 16)
        part = lax.dynamic_slice_in_dim(checks[0], 16 * target, 16, 1)
        if s:
            part = lax.ppermute(part, ROW, [(k, (k + s) % 16) for k in range(PANELS)])
        source = lax.rem(p - s + 16, 16)
        top_piece = [jnp.where(source == k, part, top_piece[k]) for k in range(PANELS)]
    top_piece = jnp.concatenate(top_piece)
    col_got, top_piece = lax.optimization_barrier((col_got, top_piece))

    check_piece = lax.dynamic_slice_in_dim(checks, q * 16, 16, 2)
    panel, lost, lead_send = call(
        rebuild_kernel,
        [(9, 16, 256), (6, 16, 256), (16, 3, 16, 256)],
        [col_got, check_piece],
    )
    row_panel = lax.all_gather(panel, COL)
    lost_all = lax.all_gather(lost, COL)

    swap = [(i * 16 + j, j * 16 + i) for i in range(16) for j in range(16)]
    col_piece = lax.ppermute(panel, ROW + COL, swap)
    lead_rows = exchange(lead_send, ROW)
    lead_rows, col_piece = lax.optimization_barrier((lead_rows, col_piece))
    (half_send,) = call(
        lead_half_kernel, [(16, 6, 8, 256)], [core_arg, lead_rows[:PANELS]], [SMEM, VMEM]
    )
    lead_mine = exchange(half_send, COL)
    lead_other = lax.ppermute(lead_mine, "core", [(0, 1), (1, 0)])

    both = jnp.concatenate([col_piece, top_piece])
    both, lead_mine, row_panel = lax.optimization_barrier((both, lead_mine, row_panel))
    mine = exchange(jnp.broadcast_to(both[None], (8, *both.shape)), "xy")

    off, inv = call(
        lead_kernel,
        [(PANELS, 256, 256)] * 2,
        [core_arg, lead_mine, lead_other],
        [SMEM, VMEM, VMEM],
        [(6, 256, 256)],
        2 * 10**10,
    )

    mine, inv = lax.optimization_barrier((mine, inv))
    other = lax.ppermute(mine, "core", [(0, 1), (1, 0)])

    totals, x3, y3 = call(
        solve_kernel,
        [(3, 3, 256, 256)],
        [core_arg, row_panel, mine, other, checks, off, inv],
        [SMEM] + [VMEM] * 6,
        [(9, 256, 256)] * 2,
        3 * 10**9,
        halves_outs=[(3, 256, 2304)] * 2,
        halves_scratch=[(3, 2304, 256), (6, 256, 768)],
        limit=32,
    )

    missing = col_got[0, 96, 0].astype(jnp.int32)
    place = jnp.stack([p, q, missing]).astype(jnp.int32)
    (factored,) = call(
        finish_kernel,
        [(4608, 128)],
        [place, lost_all, block, x3, y3],
        [SMEM] + [VMEM] * 4,
    )
    totals = totals.transpose(0, 2, 1, 3).reshape(checksum.shape)
    return (factored.reshape(matrix.shape), totals)


def solution(mesh):
    finer = Mesh(mesh.devices.reshape(8, 2, 2, 8), ("xy", "core", "col_0", "col_1"))
    in_specs = (P(ROW, None, None, COL, None, None), P(ROW, None, None, None, None), P(COL))
    out_specs = (P(ROW, None, None, COL, None, None), P(ROW, None, None, None, None))
    return jax.shard_map(
        shards, mesh=finer, in_specs=in_specs, out_specs=out_specs, check_vma=False
    )
```
